32 devices in a mesh: groups: 2 (over x), expert: 16 (over z, y, core).
Axes of the slice: x: 2, y: 2, z: 4, core: 2. Of those that a mesh axis runs over, the one named last changes fastest.
Arguments:
- residual: bfloat16 [1024, 2880], P(('groups', 'expert')), parts along dimension 0, may hold values from -6 to 6
- norm_gain: float32 [2880], replicated, may hold values from 0.1 to 1.9
- expert_ids: int32 [1024, 4], P(('groups', 'expert')), parts along dimension 0, may hold values from 0 to 7, all different within a row; in each aligned block of 32 rows (0 to 31, 32 to 63, ...) at most 32 rows name the same one
- route_logits: float32 [1024, 4], P(('groups', 'expert')), parts along dimension 0, may hold values from -6 to 6
- w_gate_up: bfloat16 [16, 2880, 1536], P('expert'), may hold values from -0.109375 to 0.109375
- w_down: bfloat16 [16, 768, 2880], P('expert'), may hold values from -0.15625 to 0.15625
Outputs:
- layer_out: bfloat16 [1024, 2880], P(('groups', 'expert')), parts along dimension 0
The draws below stay inside these ranges and needn't reach their ends.
There are 2 independent parts, one for each index of `groups`. The reference program is written for one: setup_inputs(seed, part) draws one part's arguments, and reference() takes and returns one part's arrays. A program takes and returns all parts, laid end to end along the dimension named above; an argument that names none is the same for every part. Nothing has to cross between parts.
Inputs may be any that keep to these rules, and one draw needn't show every extreme that they name: `expert_ids`: in each aligned block of 32 tokens no expert is named by more than 32 routes, and some expert reaches 32 in some block; the 4 experts of a token differ.
All inputs are finite; a program needn't handle non-finite values.
Results may differ from the reference program's by a relative error of at most 0.0062.
Values may be sent and summed in bfloat16 or wider, within the bound.
No kernel may reach another device: no remote copies, remote signals or barrier semaphores. Data moves between devices by JAX's collectives and lax.ppermute only.
A program may use at most 64 MiB of HBM per device.

```python
import math
import jax
import jax.numpy as jnp
import numpy as np
from jax import lax

D = 2880
TOP = 4
FF = 1536
FF_DEV = 768
TOK_DEV = 32
EXPERTS = 8
CAP = 32
TOKENS = 512
N_EXPERT = 16


def steps_of(key, shape, pieces, low, high):
    loudness, own = 1.0, jax.random.fold_in(key, 6)
    for axis_at, shards_of in pieces:
        draws = jnp.exp(jax.random.uniform(jax.random.fold_in(own, axis_at), (shards_of,), jnp.float32, low / len(pieces), high / len(pieces)))
        loudness = loudness * jnp.repeat(draws, shape[axis_at] // shards_of).reshape([-1 if axis == axis_at else 1 for axis in range(len(shape))])
    return loudness


def routed_block(own_key, own, number, rows, amount, top, most, slope):
    sequence = jax.random.permutation(own_key, amount)
    heavy_load, ordinary = load_shares(amount, rows * top, most, slope, True), load_shares(amount, rows * top, most, slope, False)
    places = jnp.arange(amount)

    def named(tallies, offset_by):
        used = int((tallies > 0).sum())
        fixed = max(1, used // 4)
        moved = fixed + (places - fixed + offset_by * (used - fixed)) % max(1, amount - fixed)
        return jnp.zeros((amount,), jnp.int32).at[sequence[jnp.where(places < fixed, places, moved)]].set(jnp.asarray(tallies, jnp.int32))

    tallies = jnp.where(number % 4 == 0, named(heavy_load, number // 4), named(ordinary, number - number // 4 - 1))
    mixed = jax.random.permutation(jax.random.fold_in(own, 3), amount)
    donor, taker = mixed[0:amount // 2 * 2:2], mixed[1:amount // 2 * 2:2]
    margin = jnp.minimum(tallies[donor] - 1, most - tallies[taker]) // 2
    margin = jnp.where((donor == sequence[0]) | (taker == sequence[0]) | (tallies[taker] == 0), 0, jnp.maximum(margin, 0))
    moved = jax.random.randint(jax.random.fold_in(own, 4), (amount // 2,), 0, 1 << 20) % (margin + 1)
    tallies = tallies.at[donor].add(-moved).at[taker].add(moved)
    items = jnp.searchsorted(jnp.cumsum(tallies), jnp.arange(rows * top), side="right").astype(jnp.int32)
    listing = items.reshape(top, rows).T
    listing = listing[jax.random.permutation(jax.random.fold_in(own, 1), rows)]
    offset_by = jax.random.randint(jax.random.fold_in(own, 2), (rows, 1), 0, top)
    return jnp.take_along_axis(listing, (jnp.arange(top)[None, :] + offset_by) % top, axis=1)


def load_shares(amount, total, reach, skew, full):
    loads = [(1 << 20) // math.isqrt(rank ** skew) + 1 for rank in range(1, amount + 1)]
    largest = reach if full else min(reach, max(-(-total // amount), total * loads[0] // sum(loads)))
    least = 1 if total - largest >= amount - 1 else 0
    holding, spare = [largest] + [least] * (amount - 1), total - largest - least * (amount - 1)
    while spare > 0:
        candidates = [i for i in range(1, amount) if holding[i] < largest] or [i for i in range(1, amount) if holding[i] < reach]
        mass, left = sum([loads[i] for i in candidates]), spare
        for i in candidates:
            extra = min(reach - holding[i], max(1, left * loads[i] // mass), spare)
            holding[i] = holding[i] + extra
            spare = spare - extra
    return np.array(holding)


def noise(stream_key, extent, spread, limit, shards=(), held_as=jnp.bfloat16):
    loudness = steps_of(stream_key, extent, shards, -0.22, 0.18) if shards else 1.0
    drawn = jax.random.normal(stream_key, extent, jnp.float32) * spread * loudness
    return jnp.minimum(jnp.maximum(drawn, -limit), limit).astype(held_as)


def setup_inputs(seed: int = 0, part: int = 0) -> dict:
    streams_of = jax.random.split(jax.random.key(seed), 7)
    part_splits = jax.random.split(jax.random.fold_in(streams_of[6], part), 7)
    residual = noise(part_splits[0], (TOKENS, D), 1.0, 6.0, ((0, 16),))
    norm_gain = jnp.clip(1.0 + 0.18 * jax.random.normal(streams_of[1], (D,), jnp.float32), 0.1, 1.9)
    expert_ids_keys = jax.random.split(jax.random.fold_in(part_splits[2], 1), TOKENS // TOK_DEV)
    expert_ids_turns = jax.random.permutation(jax.random.fold_in(part_splits[2], 3), TOKENS // TOK_DEV)
    expert_ids = jax.vmap(lambda own, number: routed_block(jax.random.fold_in(part_splits[2], 2), own, number, TOK_DEV, EXPERTS, TOP, CAP, 2))(expert_ids_keys, expert_ids_turns).reshape((TOKENS, TOP))
    route_logits = noise(part_splits[3], (TOKENS, TOP), 1.5, 6.0, ((0, 16),), jnp.float32)
    w_gate_up = noise(streams_of[4], (2 * EXPERTS, D, 2 * FF_DEV), D ** -0.5, 0.109375, ((0, 16),))
    w_down = noise(streams_of[5], (2 * EXPERTS, FF_DEV, D), FF ** -0.5, 0.15625, ((0, 16),))
    return {"residual": residual, "norm_gain": norm_gain, "expert_ids": expert_ids, "route_logits": route_logits, "w_gate_up": w_gate_up, "w_down": w_down}


def rms_scale(hidden, gain):
    values = hidden.astype(jnp.float32)
    meansq = lax.optimization_barrier(jnp.mean(values * values, axis=-1, keepdims=True))
    return (values * lax.rsqrt(meansq + 1e-05) * gain).astype(jnp.bfloat16)

def expert_half(inputs, w_up, w_dn):
    projected = jnp.dot(inputs, w_up, preferred_element_type=jnp.float32)
    gate_part = projected[:, :FF_DEV]
    up_part = projected[:, FF_DEV:]
    activated = (gate_part * jax.nn.sigmoid(1.702 * gate_part) * (up_part + 1.0)).astype(jnp.bfloat16)
    return jnp.dot(activated, w_dn, preferred_element_type=jnp.float32).astype(jnp.bfloat16)

def block_slots(flat_ids):
    onehot = (flat_ids[:, None] == jnp.arange(EXPERTS, dtype=jnp.int32)[None, :]).astype(jnp.int32)
    before = jnp.cumsum(onehot, axis=0) - onehot
    return lax.optimization_barrier(jnp.sum(before * onehot, axis=1)).astype(jnp.int32)

def reference(residual, norm_gain, expert_ids, route_logits, w_gate_up, w_down):
    hidden = residual
    normed = rms_scale(hidden, norm_gain)
    route_weights = jax.nn.softmax(route_logits.astype(jnp.float32), axis=-1)
    flat_ids = expert_ids.reshape(N_EXPERT, TOK_DEV * TOP).astype(jnp.int32)
    slots = jax.vmap(block_slots)(flat_ids)
    routed = jnp.repeat(normed, TOP, axis=0).reshape(N_EXPERT, TOK_DEV * TOP, D)

    def fill(ids_block, slot_block, row_block):
        return jnp.zeros((EXPERTS, CAP, D), jnp.bfloat16).at[ids_block, slot_block].set(row_block)
    buffers = jax.vmap(fill)(flat_ids, slots, routed)

    def one_expert(expert):
        inputs = buffers[:, expert].reshape(N_EXPERT * CAP, D)
        first = expert_half(inputs, w_gate_up[2 * expert], w_down[2 * expert])
        second = expert_half(inputs, w_gate_up[2 * expert + 1], w_down[2 * expert + 1])
        summed = (first.astype(jnp.float32) + second.astype(jnp.float32)).astype(jnp.bfloat16)
        return summed.reshape(N_EXPERT, CAP, D)
    results = lax.map(one_expert, jnp.arange(EXPERTS, dtype=jnp.int32))
    sources = jnp.repeat(jnp.arange(N_EXPERT, dtype=jnp.int32), TOK_DEV * TOP)
    picked = results[flat_ids.reshape(-1), sources, slots.reshape(-1)]
    picked = picked.astype(jnp.float32).reshape(TOKENS, TOP, D)
    combined = lax.optimization_barrier(jnp.sum(picked * route_weights[..., None], axis=1))
    return (hidden.astype(jnp.float32) + combined).astype(jnp.bfloat16)
```

```python
import jax
import jax.numpy as jnp
from jax import lax
from jax.sharding import PartitionSpec as P

LANES = 128


def rms_scale(hidden, gain):
    values = hidden.astype(jnp.float32)
    meansq = jnp.mean(values * values, axis=-1, keepdims=True)
    return (values * lax.rsqrt(meansq + 1e-05) * gain).astype(jnp.bfloat16)


def swap(x, mask):
    n = lax.axis_size("expert")
    return lax.ppermute(x, "expert", [(i, i ^ mask) for i in range(n)])


def gather_blocks(own):
    n = lax.axis_size("expert")
    blocks = {0: own}
    if n == 16:
        blocks[4] = swap(own, 4)
        blocks[12] = swap(own, 12)
        blocks[2] = swap(own, 2)
        blocks[6] = swap(blocks[4], 2)
        blocks[8] = swap(blocks[12], 4)
        blocks[14] = swap(blocks[12], 2)
        blocks[10] = swap(blocks[8], 2)
    else:
        mask = n // 2
        while mask > 1:
            for r in list(blocks):
                blocks[r ^ mask] = swap(blocks[r], mask)
            mask //= 2
    for r in list(blocks):
        blocks[r ^ 1] = swap(blocks[r], 1)
    return blocks


def add(*terms):
    total = terms[0].astype(jnp.float32)
    for term in terms[1:]:
        total = total + term.astype(jnp.float32)
    return total.astype(jnp.bfloat16)


def scatter_sum(parts):
    n = lax.axis_size("expert")
    parts = {r: add(parts[r], swap(parts[r ^ 1], 1)) for r in parts if not r & 1}
    if n == 16:
        parts = {r: add(parts[r], swap(parts[r ^ 2], 2)) for r in (8, 12, 4, 0)}
        far = add(parts[12], swap(parts[8], 4))
        return parts[0], swap(parts[4], 4), swap(far, 12)
    mask = 2
    while mask < n:
        parts = {r: add(parts[r], swap(parts[r ^ mask], mask)) for r in parts if not r & mask}
        mask *= 2
    return (parts[0],)


def local(residual, norm_gain, expert_ids, route_logits, w_gate_up, w_down):
    tokens, width = residual.shape
    n = lax.axis_size("expert")
    experts = n // 2
    half_units = w_down.shape[1]
    normed = rms_scale(residual, norm_gain)
    route_weights = jax.nn.softmax(route_logits, axis=-1)
    named = expert_ids[:, :, None] == jnp.arange(experts, dtype=jnp.int32)
    by_expert = jnp.sum(jnp.where(named, route_weights[:, :, None], 0.0), axis=1)
    high = by_expert.astype(jnp.bfloat16)
    low = (by_expert - high.astype(jnp.float32)).astype(jnp.bfloat16)
    filler = -(width + 2 * experts) % LANES
    own = jnp.concatenate([normed, high, low, jnp.zeros((tokens, filler), jnp.bfloat16)], axis=1)

    blocks = gather_blocks(own)
    order = sorted(blocks)
    rows = jnp.concatenate([blocks[r] for r in order], axis=0)
    mine = lax.axis_index("expert") // 2
    column = jnp.arange(2 * experts, dtype=jnp.int32) % experts
    tail = rows[:, width : width + 2 * experts].astype(jnp.float32)
    weight = jnp.sum(jnp.where(column == mine, tail, 0.0), axis=1, keepdims=True)
    projected = jnp.dot(rows[:, :width], w_gate_up[0], preferred_element_type=jnp.float32)
    a = projected[:, :half_units]
    b = projected[:, half_units:]
    act = (a * jax.nn.sigmoid(1.702 * a) * (b + 1.0) * weight).astype(jnp.bfloat16)
    out = jnp.dot(act, w_down[0], preferred_element_type=jnp.float32).astype(jnp.bfloat16)
    parts = {r: out[k * tokens : (k + 1) * tokens] for k, r in enumerate(order)}
    return add(residual, *scatter_sum(parts))


def solution(mesh):
    placed = (
        P(("groups", "expert"), None),
        P(),
        P(("groups", "expert"), None),
        P(("groups", "expert"), None),
        P("expert", None, None),
        P("expert", None, None),
    )
    return jax.shard_map(
        local, mesh=mesh, in_specs=placed, out_specs=P(("groups", "expert"), None), check_vma=False
    )
```

```python
import functools

import jax
import jax.numpy as jnp
from jax import lax
from jax.experimental import pallas as pl
from jax.experimental.pallas import tpu as pltpu
from jax.sharding import PartitionSpec as P

LANES = 128
VMEM = pl.BlockSpec(memory_space=pltpu.VMEM)
HBM = pl.BlockSpec(memory_space=pltpu.HBM)
SMEM = pl.BlockSpec(memory_space=pltpu.SMEM)


def in_hbm(*arrays):
    return [pltpu.with_memory_space_constraint(x, pltpu.HBM) for x in arrays]


def pack_kernel(experts, _, residual_hbm, gain_hbm, ids_hbm, logits_hbm, out_ref, residual_ref, gain_ref, ids_ref, logits_ref, sems):
    copies = [
        pltpu.make_async_copy(ids_hbm, ids_ref, sems.at[0]),
        pltpu.make_async_copy(logits_hbm, logits_ref, sems.at[1]),
        pltpu.make_async_copy(residual_hbm, residual_ref, sems.at[2]),
        pltpu.make_async_copy(gain_hbm, gain_ref.at[0], sems.at[3]),
    ]
    for copy in copies:
        copy.start()
    tokens, width = residual_ref.shape
    spare = out_ref.shape[1] - width
    copies[0].wait()
    copies[1].wait()
    logits = logits_ref[...]
    grown = jnp.exp(logits - jnp.max(logits, axis=0, keepdims=True))
    weights = grown / jnp.sum(grown, axis=0, keepdims=True)
    ids = ids_ref[...]
    by_expert = jnp.concatenate(
        [jnp.sum(jnp.where(ids == e, weights, 0.0), axis=0, keepdims=True) for e in range(experts)],
        axis=0,
    )
    high = by_expert.astype(jnp.bfloat16).astype(jnp.float32)
    blank = jnp.zeros((spare - 2 * experts, tokens), jnp.float32)
    columns = jnp.concatenate([high, by_expert - high, blank], axis=0).astype(jnp.bfloat16)
    row = lax.broadcasted_iota(jnp.int32, (tokens, tokens), 0)
    eye = (row == lax.broadcasted_iota(jnp.int32, (tokens, tokens), 1)).astype(jnp.bfloat16)
    tail = lax.dot_general(
        eye, columns, (((1,), (1,)), ((), ())), preferred_element_type=jnp.float32
    ).astype(jnp.bfloat16)
    copies[2].wait()
    copies[3].wait()
    values = residual_ref[...].astype(jnp.float32)
    meansq = jnp.mean(values * values, axis=-1, keepdims=True)
    normed = (values * lax.rsqrt(meansq + 1e-05) * gain_ref[...]).astype(jnp.bfloat16)
    out_ref[...] = jnp.concatenate([normed, tail], axis=1)


def pack(mine, residual, gain, ids, logits, experts):
    tokens, width = residual.shape
    top = ids.shape[1]
    padded = -(-(width + 2 * experts) // LANES) * LANES
    return pl.pallas_call(
        functools.partial(pack_kernel, experts),
        out_shape=jax.ShapeDtypeStruct((tokens, padded), jnp.bfloat16),
        in_specs=[SMEM] + [HBM] * 4,
        out_specs=VMEM,
        scratch_shapes=[
            pltpu.VMEM((tokens, width), jnp.bfloat16),
            pltpu.VMEM((1, width), jnp.float32),
            pltpu.VMEM((top, tokens), jnp.int32),
            pltpu.VMEM((top, tokens), jnp.float32),
            pltpu.SemaphoreType.DMA((4,)),
        ],
        compiler_params=pltpu.CompilerParams(vmem_limit_bytes=8 << 20),
        name="pack",
    )(mine, *in_hbm(residual, gain, ids.T, logits.T))


def again_kernel(source, target):
    target[...] = source[...]


def again(x):
    return pl.pallas_call(
        again_kernel,
        out_shape=jax.ShapeDtypeStruct(x.shape, x.dtype),
        in_specs=[VMEM],
        out_specs=VMEM,
        compiler_params=pltpu.CompilerParams(vmem_limit_bytes=2 << 20),
        name="again",
    )(x)


def load_kernel(*refs):
    source, _, target, mark, sem = refs
    copy = pltpu.make_async_copy(source, target, sem)
    copy.start()
    mark[...] = jnp.zeros_like(mark)
    copy.wait()


def load(after, weight):
    return pl.pallas_call(
        load_kernel,
        out_shape=[
            pltpu.VMEM(weight.shape, weight.dtype),
            jax.ShapeDtypeStruct((8, LANES), jnp.float32),
        ],
        in_specs=[HBM, pl.BlockSpec(memory_space=pl.ANY)],
        out_specs=[VMEM] * 2,
        scratch_shapes=[pltpu.SemaphoreType.DMA(())],
        compiler_params=pltpu.CompilerParams(vmem_limit_bytes=1 << 20),
        cost_estimate=pl.CostEstimate(
            flops=0, bytes_accessed=2 * weight.size, transcendentals=0
        ),
        name="load",
    )(*in_hbm(weight), after)


def mlp_kernel(experts, count, mine_ref, mark_ref, *refs):
    blocks, (w_up, w_dn) = refs[:count], refs[count : count + 2]
    even_ref, odd_ref, rows, act = refs[count + 2 :]
    width, half = w_dn.shape
    tokens = even_ref.shape[1]
    views = [b.at[k] for b in blocks for k in range(b.shape[0])]
    for k, view in enumerate(views):
        rows[pl.ds(k * tokens, tokens), :] = view[...]
    tail = rows[:, width : width + 2 * experts].astype(jnp.float32)
    column = lax.rem(lax.broadcasted_iota(jnp.int32, (1, 2 * experts), 1), experts)
    weight = jnp.sum(jnp.where(column == mine_ref[0], tail, 0.0), axis=1, keepdims=True)
    x = rows[:, :width]
    step = 256 if half % 256 == 0 else half
    for at in range(0, half, step):
        a = jnp.dot(x, w_up[:, at : at + step], preferred_element_type=jnp.float32)
        b = jnp.dot(x, w_up[:, half + at : half + at + step], preferred_element_type=jnp.float32)
        act[:, at : at + step] = (a * jax.nn.sigmoid(1.702 * a) * (b + 1.0) * weight).astype(
            jnp.bfloat16
        )
    out = lax.dot_general(
        act[...], w_dn[...], (((1,), (1,)), ((), ())), preferred_element_type=jnp.float32
    ).astype(jnp.bfloat16)
    for k in range(len(views)):
        ref = (even_ref, odd_ref)[2 * k // len(views)]
        ref[k % ref.shape[0]] = out[k * tokens : (k + 1) * tokens]


def mlp(blocks, mine, mark, w_up, w_dn, experts):
    count, number, tokens = len(blocks), sum(b.shape[0] for b in blocks), blocks[0].shape[1]
    m = number * tokens
    width, half = w_dn.shape
    return pl.pallas_call(
        functools.partial(mlp_kernel, experts, count),
        out_shape=[jax.ShapeDtypeStruct((number // 2, tokens, width), jnp.bfloat16)] * 2,
        in_specs=[SMEM, pl.BlockSpec(memory_space=pl.ANY)] + [VMEM] * (count + 2),
        out_specs=[VMEM] * 2,
        scratch_shapes=[
            pltpu.VMEM((m, blocks[0].shape[2]), jnp.bfloat16),
            pltpu.VMEM((m, half), jnp.bfloat16),
        ],
        compiler_params=pltpu.CompilerParams(vmem_limit_bytes=24 << 20),
        cost_estimate=pl.CostEstimate(
            flops=6 * m * width * half, bytes_accessed=6 * width * half, transcendentals=m * half
        ),
        name="mlp",
    )(mine, mark, *blocks, *[pltpu.with_memory_space_constraint(w, pltpu.VMEM) for w in (w_up, w_dn)])


def swap(x, mask):
    n = lax.axis_size("expert")
    return lax.ppermute(x, "expert", [(i, i ^ mask) for i in range(n)])


def add(*terms):
    total = terms[0].astype(jnp.float32)
    for term in terms[1:]:
        total = total + term.astype(jnp.float32)
    return total.astype(jnp.bfloat16)


def local(residual, norm_gain, expert_ids, route_logits, w_gate_up, w_down):
    n = lax.axis_size("expert")
    tokens = residual.shape[0]
    experts = n // 2
    mine = lax.div(lax.axis_index("expert"), 2).reshape(1)
    own = pack(mine, residual, norm_gain, expert_ids, route_logits, experts)
    def terms(mixed, other):
        return mlp([mixed, other], mine, mark, w_up, w_dn, experts)

    w_dn, mark = load(own, w_down[0].T)
    if n == 16:
        together = lax.optimization_barrier
        far = swap(own, 8)
        copied = again(own)
        near = swap(copied, 4)
        side = swap(copied, 2)
        near, side, mark = together((near, side, mark))
        near_side = swap(near, 2)
        w_up, mark = load(mark, w_gate_up[0])
        far, mark = together((far, mark))
        last = swap(far, 4)
        mixed = jnp.stack((own, near, side, near_side))
        mixed, far = together((mixed, far))
        far_side = swap(far, 2)
        even, odd = terms(mixed, swap(mixed, 1))
        last, far_side, even = together((last, far_side, even))
        last_side = swap(last, 2)
        far_mixed = jnp.stack((far, far_side))
        far_even, far_odd = terms(far_mixed, swap(far_mixed, 1))
        last_side, far_even = together((last_side, far_even))
        last_mixed = jnp.stack((last, last_side))
        last_even, last_odd = terms(last_mixed, swap(last_mixed, 1))

        odd, far_odd, last_odd = swap(odd, 1), swap(far_odd, 1), swap(last_odd, 1)
        near_away = swap(add(even[3], odd[3]), 2)
        far_send, near_away = together((add(far_even[1], far_odd[1]), near_away))
        near_sum = add(even[1], odd[1], near_away)
        near_back = swap(near_sum, 4)
        far_sum = add(far_even[0], far_odd[0], swap(far_send, 2))
        last_away = swap(add(last_even[1], last_odd[1]), 2)
        own_send, last_away, near_back = together((add(even[2], odd[2]), last_away, near_back))
        last_sum = add(last_even[0], last_odd[0], last_away)
        return add(
            residual,
            even[0],
            odd[0],
            swap(own_send, 2),
            near_back,
            swap(far_sum, 8),
            swap(last_sum, 12),
        )
    w_up, mark = load(mark, w_gate_up[0])
    blocks = {0: own}
    mask = n // 2
    while mask > 1:
        for r in list(blocks):
            blocks[r ^ mask] = swap(blocks[r], mask)
        mask //= 2
    parts = {}
    for r in sorted(blocks):
        mixed = blocks[r][None]
        even, odd = terms(mixed, swap(mixed, 1))
        parts[r] = add(even, swap(odd, 1))[0]
    mask = 2
    while mask < n:
        parts = {r: add(parts[r], swap(parts[r ^ mask], mask)) for r in parts if not r & mask}
        mask *= 2
    return add(residual, parts[0])


def solution(mesh):
    placed = (
        P(("groups", "expert"), None),
        P(),
        P(("groups", "expert"), None),
        P(("groups", "expert"), None),
        P("expert", None, None),
        P("expert", None, None),
    )
    return jax.shard_map(
        local, mesh=mesh, in_specs=placed, out_specs=P(("groups", "expert"), None), check_vma=False
    )
```

```python
import functools

import jax
import jax.numpy as jnp
from jax import lax
from jax.experimental import pallas as pl
from jax.experimental.pallas import tpu as pltpu
from jax.sharding import PartitionSpec as P

LANES = 128
VMEM = pl.BlockSpec(memory_space=pltpu.VMEM)
HBM = pl.BlockSpec(memory_space=pltpu.HBM)
SMEM = pl.BlockSpec(memory_space=pltpu.SMEM)


def in_hbm(*arrays):
    return [pltpu.with_memory_space_constraint(x, pltpu.HBM) for x in arrays]


def pack_kernel(experts, _, residual_hbm, gain_hbm, ids_hbm, logits_hbm, out_ref, residual_ref, gain_ref, ids_ref, logits_ref, sems):
    copies = [
        pltpu.make_async_copy(ids_hbm, ids_ref, sems.at[0]),
        pltpu.make_async_copy(logits_hbm, logits_ref, sems.at[1]),
        pltpu.make_async_copy(residual_hbm, residual_ref, sems.at[2]),
        pltpu.make_async_copy(gain_hbm, gain_ref.at[0], sems.at[3]),
    ]
    for copy in copies:
        copy.start()
    tokens, width = residual_ref.shape
    spare = out_ref.shape[1] - width
    copies[0].wait()
    copies[1].wait()
    logits = logits_ref[...]
    grown = jnp.exp(logits - jnp.max(logits, axis=0, keepdims=True))
    weights = grown / jnp.sum(grown, axis=0, keepdims=True)
    ids = ids_ref[...]
    by_expert = jnp.concatenate(
        [jnp.sum(jnp.where(ids == e, weights, 0.0), axis=0, keepdims=True) for e in range(experts)],
        axis=0,
    )
    high = by_expert.astype(jnp.bfloat16).astype(jnp.float32)
    blank = jnp.zeros((spare - 2 * experts, tokens), jnp.float32)
    columns = jnp.concatenate([high, by_expert - high, blank], axis=0).astype(jnp.bfloat16)
    row = lax.broadcasted_iota(jnp.int32, (tokens, tokens), 0)
    eye = (row == lax.broadcasted_iota(jnp.int32, (tokens, tokens), 1)).astype(jnp.bfloat16)
    tail = lax.dot_general(
        eye, columns, (((1,), (1,)), ((), ())), preferred_element_type=jnp.float32
    ).astype(jnp.bfloat16)
    copies[2].wait()
    copies[3].wait()
    values = residual_ref[...].astype(jnp.float32)
    meansq = jnp.mean(values * values, axis=-1, keepdims=True)
    normed = (values * lax.rsqrt(meansq + 1e-05) * gain_ref[...]).astype(jnp.bfloat16)
    out_ref[...] = jnp.concatenate([normed, tail], axis=1)


def pack(mine, residual, gain, ids, logits, experts):
    tokens, width = residual.shape
    top = ids.shape[1]
    padded = -(-(width + 2 * experts) // LANES) * LANES
    return pl.pallas_call(
        functools.partial(pack_kernel, experts),
        out_shape=jax.ShapeDtypeStruct((tokens, padded), jnp.bfloat16),
        in_specs=[SMEM] + [HBM] * 4,
        out_specs=VMEM,
        scratch_shapes=[
            pltpu.VMEM((tokens, width), jnp.bfloat16),
            pltpu.VMEM((1, width), jnp.float32),
            pltpu.VMEM((top, tokens), jnp.int32),
            pltpu.VMEM((top, tokens), jnp.float32),
            pltpu.SemaphoreType.DMA((4,)),
        ],
        compiler_params=pltpu.CompilerParams(vmem_limit_bytes=8 << 20),
        name="pack",
    )(mine, *in_hbm(residual, gain, ids.T, logits.T))


def load_kernel(*refs):
    source, _, target, mark, sem = refs
    copy = pltpu.make_async_copy(source, target, sem)
    copy.start()
    mark[...] = jnp.zeros_like(mark)
    copy.wait()


def load(after, weight):
    return pl.pallas_call(
        load_kernel,
        out_shape=[
            pltpu.VMEM(weight.shape, weight.dtype),
            jax.ShapeDtypeStruct((8, LANES), jnp.float32),
        ],
        in_specs=[HBM, pl.BlockSpec(memory_space=pl.ANY)],
        out_specs=[VMEM] * 2,
        scratch_shapes=[pltpu.SemaphoreType.DMA(())],
        compiler_params=pltpu.CompilerParams(vmem_limit_bytes=1 << 20),
        cost_estimate=pl.CostEstimate(
            flops=0, bytes_accessed=2 * weight.size, transcendentals=0
        ),
        name="load",
    )(*in_hbm(weight), after)


def mlp_kernel(experts, count, mine_ref, mark_ref, *refs):
    blocks, (w_up, w_dn) = refs[:count], refs[count : count + 2]
    even_ref, odd_ref, rows, act = refs[count + 2 :]
    width, half = w_dn.shape
    tokens = even_ref.shape[1]
    views = [b.at[k] for b in blocks for k in range(b.shape[0])]
    for k, view in enumerate(views):
        rows[pl.ds(k * tokens, tokens), :] = view[...]
    tail = rows[:, width : width + 2 * experts].astype(jnp.float32)
    column = lax.rem(lax.broadcasted_iota(jnp.int32, (1, 2 * experts), 1), experts)
    weight = jnp.sum(jnp.where(column == mine_ref[0], tail, 0.0), axis=1, keepdims=True)
    x = rows[:, :width]
    step = 256 if half % 256 == 0 else half
    for at in range(0, half, step):
        a = jnp.dot(x, w_up[:, at : at + step], preferred_element_type=jnp.float32)
        b = jnp.dot(x, w_up[:, half + at : half + at + step], preferred_element_type=jnp.float32)
        act[:, at : at + step] = (a * jax.nn.sigmoid(1.702 * a) * (b + 1.0) * weight).astype(
            jnp.bfloat16
        )
    out = lax.dot_general(
        act[...], w_dn[...], (((1,), (1,)), ((), ())), preferred_element_type=jnp.float32
    ).astype(jnp.bfloat16)
    for k in range(len(views)):
        ref = (even_ref, odd_ref)[2 * k // len(views)]
        ref[k % ref.shape[0]] = out[k * tokens : (k + 1) * tokens]


def mlp(blocks, mine, mark, w_up, w_dn, experts):
    count, number, tokens = len(blocks), sum(b.shape[0] for b in blocks), blocks[0].shape[1]
    m = number * tokens
    width, half = w_dn.shape
    return pl.pallas_call(
        functools.partial(mlp_kernel, experts, count),
        out_shape=[jax.ShapeDtypeStruct((number // 2, tokens, width), jnp.bfloat16)] * 2,
        in_specs=[SMEM, pl.BlockSpec(memory_space=pl.ANY)] + [VMEM] * (count + 2),
        out_specs=[VMEM] * 2,
        scratch_shapes=[
            pltpu.VMEM((m, blocks[0].shape[2]), jnp.bfloat16),
            pltpu.VMEM((m, half), jnp.bfloat16),
        ],
        compiler_params=pltpu.CompilerParams(vmem_limit_bytes=24 << 20),
        cost_estimate=pl.CostEstimate(
            flops=6 * m * width * half, bytes_accessed=6 * width * half, transcendentals=m * half
        ),
        name="mlp",
    )(mine, mark, *blocks, *[pltpu.with_memory_space_constraint(w, pltpu.VMEM) for w in (w_up, w_dn)])


def swap(x, mask):
    n = lax.axis_size("expert")
    return lax.ppermute(x, "expert", [(i, i ^ mask) for i in range(n)])


def add(*terms):
    total = terms[0].astype(jnp.float32)
    for term in terms[1:]:
        total = total + term.astype(jnp.float32)
    return total.astype(jnp.bfloat16)


def local(residual, norm_gain, expert_ids, route_logits, w_gate_up, w_down):
    n = lax.axis_size("expert")
    tokens = residual.shape[0]
    experts = n // 2
    mine = lax.div(lax.axis_index("expert"), 2).reshape(1)
    own = pack(mine, residual, norm_gain, expert_ids, route_logits, experts)
    def terms(mixed, other):
        return mlp([mixed, other], mine, mark, w_up, w_dn, experts)

    w_dn, mark = load(own, w_down[0].T)
    if n == 16:
        together = lax.optimization_barrier
        far = swap(own, 8)
        near = swap(own, 4)
        side = swap(own, 2)
        near, side, mark = together((near, side, mark))
        near_side = swap(near, 2)
        w_up, mark = load(mark, w_gate_up[0])
        far, mark = together((far, mark))
        last = swap(far, 4)
        mixed = jnp.stack((own, side, near, near_side))
        mixed, far = together((mixed, far))
        far_side = swap(far, 2)
        even, odd = terms(mixed, swap(mixed, 1))
        last, far_side, even = together((last, far_side, even))
        last_side = swap(last, 2)
        far_mixed = jnp.stack((far, far_side))
        far_other = swap(far_mixed, 1)
        first = add(even, swap(odd, 1))
        far_even, far_odd = terms(far_mixed, far_other)
        last_side, far_even = together((last_side, far_even))
        last_mixed = jnp.stack((last, last_side))
        last_other = swap(last_mixed, 1)
        far_sums = add(far_even, swap(far_odd, 1))
        far_send = far_sums[1]
        crossed = swap(first[2:], 4)
        last_even, last_odd = terms(last_mixed, last_other)
        last_sums = add(last_even, swap(last_odd, 1))
        last_send = last_sums[1]
        far_away = swap(far_send, 2)
        last_away = swap(last_send, 2)
        relayed = swap(add(far_sums[0], far_away), 4)
        joined = add(last_sums[0], last_away, relayed)
        own_send = add(first[1], crossed[1])
        own_away = swap(own_send, 2)
        last_back = swap(joined, 12)
        return add(residual, first[0], crossed[0], own_away, last_back)
    w_up, mark = load(mark, w_gate_up[0])
    blocks = {0: own}
    mask = n // 2
    while mask > 1:
        for r in list(blocks):
            blocks[r ^ mask] = swap(blocks[r], mask)
        mask //= 2
    parts = {}
    for r in sorted(blocks):
        mixed = blocks[r][None]
        even, odd = terms(mixed, swap(mixed, 1))
        parts[r] = add(even, swap(odd, 1))[0]
    mask = 2
    while mask < n:
        parts = {r: add(parts[r], swap(parts[r ^ mask], mask)) for r in parts if not r & mask}
        mask *= 2
    return add(residual, parts[0])


def solution(mesh):
    placed = (
        P(("groups", "expert"), None),
        P(),
        P(("groups", "expert"), None),
        P(("groups", "expert"), None),
        P("expert", None, None),
        P("expert", None, None),
    )
    return jax.shard_map(
        local, mesh=mesh, in_specs=placed, out_specs=P(("groups", "expert"), None), check_vma=False
    )
```

```python
import functools

import jax
import jax.numpy as jnp
from jax import lax
from jax.experimental import pallas as pl
from jax.experimental.pallas import tpu as pltpu
from jax.sharding import PartitionSpec as P

LANES = 128
VMEM = pl.BlockSpec(memory_space=pltpu.VMEM)
HBM = pl.BlockSpec(memory_space=pltpu.HBM)
SMEM = pl.BlockSpec(memory_space=pltpu.SMEM)


def in_hbm(*arrays):
    return [pltpu.with_memory_space_constraint(x, pltpu.HBM) for x in arrays]


def pack_kernel(experts, _, residual_hbm, gain_hbm, ids_hbm, logits_hbm, out_ref, residual_ref, gain_ref, ids_ref, logits_ref, sems):
    copies = [
        pltpu.make_async_copy(ids_hbm, ids_ref, sems.at[0]),
        pltpu.make_async_copy(logits_hbm, logits_ref, sems.at[1]),
        pltpu.make_async_copy(residual_hbm, residual_ref, sems.at[2]),
        pltpu.make_async_copy(gain_hbm, gain_ref.at[0], sems.at[3]),
    ]
    for copy in copies:
        copy.start()
    tokens, width = residual_ref.shape
    spare = out_ref.shape[1] - width
    copies[0].wait()
    copies[1].wait()
    logits = logits_ref[...]
    grown = jnp.exp(logits - jnp.max(logits, axis=0, keepdims=True))
    weights = grown / jnp.sum(grown, axis=0, keepdims=True)
    ids = ids_ref[...]
    by_expert = jnp.concatenate(
        [jnp.sum(jnp.where(ids == e, weights, 0.0), axis=0, keepdims=True) for e in range(experts)],
        axis=0,
    )
    high = by_expert.astype(jnp.bfloat16).astype(jnp.float32)
    blank = jnp.zeros((spare - 2 * experts, tokens), jnp.float32)
    columns = jnp.concatenate([high, by_expert - high, blank], axis=0).astype(jnp.bfloat16)
    row = lax.broadcasted_iota(jnp.int32, (tokens, tokens), 0)
    eye = (row == lax.broadcasted_iota(jnp.int32, (tokens, tokens), 1)).astype(jnp.bfloat16)
    tail = lax.dot_general(
        eye, columns, (((1,), (1,)), ((), ())), preferred_element_type=jnp.float32
    ).astype(jnp.bfloat16)
    copies[2].wait()
    copies[3].wait()
    values = residual_ref[...].astype(jnp.float32)
    meansq = jnp.mean(values * values, axis=-1, keepdims=True)
    normed = (values * lax.rsqrt(meansq + 1e-05) * gain_ref[...]).astype(jnp.bfloat16)
    out_ref[...] = jnp.concatenate([normed, tail], axis=1)


def pack(mine, residual, gain, ids, logits, experts):
    tokens, width = residual.shape
    top = ids.shape[1]
    padded = -(-(width + 2 * experts) // LANES) * LANES
    return pl.pallas_call(
        functools.partial(pack_kernel, experts),
        out_shape=jax.ShapeDtypeStruct((tokens, padded), jnp.bfloat16),
        in_specs=[SMEM] + [HBM] * 4,
        out_specs=VMEM,
        scratch_shapes=[
            pltpu.VMEM((tokens, width), jnp.bfloat16),
            pltpu.VMEM((1, width), jnp.float32),
            pltpu.VMEM((top, tokens), jnp.int32),
            pltpu.VMEM((top, tokens), jnp.float32),
            pltpu.SemaphoreType.DMA((4,)),
        ],
        compiler_params=pltpu.CompilerParams(vmem_limit_bytes=8 << 20),
        name="pack",
    )(mine, *in_hbm(residual, gain, ids.T, logits.T))


def load_kernel(*refs):
    source, _, target, mark, sem = refs
    copy = pltpu.make_async_copy(source, target, sem)
    copy.start()
    mark[...] = jnp.zeros_like(mark)
    copy.wait()


def load(after, weight):
    return pl.pallas_call(
        load_kernel,
        out_shape=[
            pltpu.VMEM(weight.shape, weight.dtype),
            jax.ShapeDtypeStruct((8, LANES), jnp.float32),
        ],
        in_specs=[HBM, pl.BlockSpec(memory_space=pl.ANY)],
        out_specs=[VMEM] * 2,
        scratch_shapes=[pltpu.SemaphoreType.DMA(())],
        compiler_params=pltpu.CompilerParams(vmem_limit_bytes=1 << 20),
        cost_estimate=pl.CostEstimate(
            flops=0, bytes_accessed=2 * weight.size, transcendentals=0
        ),
        name="load",
    )(*in_hbm(weight), after)


def mlp_kernel(experts, counts, mine_ref, mark_ref, *refs):
    count = len(counts)
    blocks, (w_up, w_dn) = refs[:count], refs[count : count + 2]
    even_ref, odd_ref, rows, act = refs[count + 2 :]
    width, half = w_dn.shape
    tokens = even_ref.shape[1]
    views = [b.at[k] for b, used in zip(blocks, counts) for k in range(used)]
    for k, view in enumerate(views):
        rows[pl.ds(k * tokens, tokens), :] = view[...]
    tail = rows[:, width : width + 2 * experts].astype(jnp.float32)
    column = lax.rem(lax.broadcasted_iota(jnp.int32, (1, 2 * experts), 1), experts)
    weight = jnp.sum(jnp.where(column == mine_ref[0], tail, 0.0), axis=1, keepdims=True)
    x = rows[:, :width]
    step = 256 if half % 256 == 0 else half
    for at in range(0, half, step):
        a = jnp.dot(x, w_up[:, at : at + step], preferred_element_type=jnp.float32)
        b = jnp.dot(x, w_up[:, half + at : half + at + step], preferred_element_type=jnp.float32)
        act[:, at : at + step] = (a * jax.nn.sigmoid(1.702 * a) * (b + 1.0) * weight).astype(
            jnp.bfloat16
        )
    out = lax.dot_general(
        act[...], w_dn[...], (((1,), (1,)), ((), ())), preferred_element_type=jnp.float32
    ).astype(jnp.bfloat16)
    for k in range(len(views)):
        ref = (even_ref, odd_ref)[2 * k // len(views)]
        part = out[k * tokens : (k + 1) * tokens]
        if ref.shape[2] > width:
            filler = jnp.zeros((tokens, ref.shape[2] - width), part.dtype)
            part = jnp.concatenate([part, filler], axis=1)
        ref[k % ref.shape[0]] = part


def mlp(blocks, counts, odd_width, mine, mark, w_up, w_dn, experts):
    count, number, tokens = len(blocks), sum(counts), blocks[0].shape[1]
    m = number * tokens
    width, half = w_dn.shape
    return pl.pallas_call(
        functools.partial(mlp_kernel, experts, counts),
        out_shape=[
            jax.ShapeDtypeStruct((number // 2, tokens, columns), jnp.bfloat16)
            for columns in (width, odd_width)
        ],
        in_specs=[SMEM, pl.BlockSpec(memory_space=pl.ANY)] + [VMEM] * (count + 2),
        out_specs=[VMEM] * 2,
        scratch_shapes=[
            pltpu.VMEM((m, blocks[0].shape[2]), jnp.bfloat16),
            pltpu.VMEM((m, half), jnp.bfloat16),
        ],
        compiler_params=pltpu.CompilerParams(vmem_limit_bytes=24 << 20),
        cost_estimate=pl.CostEstimate(
            flops=6 * m * width * half, bytes_accessed=6 * width * half, transcendentals=m * half
        ),
        name="mlp",
    )(mine, mark, *blocks, *[pltpu.with_memory_space_constraint(w, pltpu.VMEM) for w in (w_up, w_dn)])


def swap(x, mask):
    n = lax.axis_size("expert")
    return lax.ppermute(x, "expert", [(i, i ^ mask) for i in range(n)])


def add(*terms):
    total = terms[0].astype(jnp.float32)
    for term in terms[1:]:
        total = total + term.astype(jnp.float32)
    return total.astype(jnp.bfloat16)


def local(residual, norm_gain, expert_ids, route_logits, w_gate_up, w_down):
    n = lax.axis_size("expert")
    tokens = residual.shape[0]
    experts = n // 2
    mine = lax.div(lax.axis_index("expert"), 2).reshape(1)
    own = pack(mine, residual, norm_gain, expert_ids, route_logits, experts)
    width = residual.shape[1]

    def terms(mixed, other, odd_width=width):
        counts = (mixed.shape[0],) * 2
        return mlp([mixed, other], counts, odd_width, mine, mark, w_up, w_dn, experts)

    w_dn, mark = load(own, w_down[0].T)
    if n == 16:
        together = lax.optimization_barrier
        far = swap(own, 8)
        near = swap(own, 4)
        side = swap(own, 2)
        near, side, mark = together((near, side, mark))
        near_side = swap(near, 2)
        w_up, mark = load(mark, w_gate_up[0])
        far, mark = together((far, mark))
        last = swap(far, 4)
        mixed = jnp.stack((own, side, near, near_side))
        mixed, far = together((mixed, far))
        far_side = swap(far, 2)
        even, odd = terms(mixed, swap(mixed, 1), own.shape[1])
        last, far_side, even = together((last, far_side, even))
        last_side = swap(last, 2)
        far_mixed = jnp.stack((far, far_side))
        far_other = swap(jnp.concatenate((far_mixed, odd)), 1)
        first = add(even, far_other[2:, :, :width])
        far_even, far_odd = terms(far_mixed, far_other)
        last_side, far_even = together((last_side, far_even))
        last_mixed = jnp.stack((last, last_side))
        last_other = swap(last_mixed, 1)
        far_sums = add(far_even, swap(far_odd, 1))
        far_send = far_sums[1]
        crossed = swap(first[3], 4)
        last_even, last_odd = terms(last_mixed, last_other)
        last_sums = add(last_even, swap(last_odd, 1))
        last_send = last_sums[1]
        far_away = swap(far_send, 2)
        last_away = swap(last_send, 2)
        far_away, crossed = together((far_away, crossed))
        relayed = swap(add(far_sums[0], far_away), 4)
        own_send = add(first[1], crossed)
        own_send, last_away = together((own_send, last_away))
        own_away = swap(own_send, 2)
        joined = add(last_sums[0], last_away, relayed)
        near_back = swap(first[2], 4)
        last_back = swap(joined, 12)
        return add(residual, first[0], near_back, own_away, last_back)
    w_up, mark = load(mark, w_gate_up[0])
    blocks = {0: own}
    mask = n // 2
    while mask > 1:
        for r in list(blocks):
            blocks[r ^ mask] = swap(blocks[r], mask)
        mask //= 2
    parts = {}
    for r in sorted(blocks):
        mixed = blocks[r][None]
        even, odd = terms(mixed, swap(mixed, 1))
        parts[r] = add(even, swap(odd, 1))[0]
    mask = 2
    while mask < n:
        parts = {r: add(parts[r], swap(parts[r ^ mask], mask)) for r in parts if not r & mask}
        mask *= 2
    return add(residual, parts[0])


def solution(mesh):
    placed = (
        P(("groups", "expert"), None),
        P(),
        P(("groups", "expert"), None),
        P(("groups", "expert"), None),
        P("expert", None, None),
        P("expert", None, None),
    )
    return jax.shard_map(
        local, mesh=mesh, in_specs=placed, out_specs=P(("groups", "expert"), None), check_vma=False
    )
```
